32 devices in a mesh: gx: 8 (over z, y), gy: 4 (over x, core).
Axes of the slice: x: 2, y: 2, z: 4, core: 2. Of those that a mesh axis runs over, the one named last changes fastest.
Arguments:
- densities: bfloat16 [8, 4, 64, 8192], P('gx', 'gy'), may hold values from -6 to 6
- trials: bfloat16 [8, 4, 64, 256], P('gx', 'gy'), may hold values from -6 to 6
- energies: float32 [8, 4, 64, 8], P('gx', 'gy'), may hold values from 1 to 4
- metric: bfloat16 [1024, 1024], replicated, may hold values from -0.1875 to 0.1875
- pair_local: int32 [8, 4, 6912], P('gx', 'gy'), may hold values from 0 to 63
- pair_remote: int32 [8, 4, 6912], P('gx', 'gy'), may hold values from 0 to 63, as said below
- pair_scale: float32 [8, 4, 6912], P('gx', 'gy'), may hold values from 0.2 to 2
Outputs:
- sigma_first: float32 [8, 4, 64, 256], P('gx', 'gy')
- corrections: bfloat16 [8, 4, 64, 256], P('gx', 'gy')
- sigma_second: float32 [8, 4, 64, 256], P('gx', 'gy')
- theta: float32 [32], replicated
The draws below stay inside these ranges and needn't reach their ends.
Inputs may be any that keep to these rules, and one draw needn't show every extreme that they name: pair_remote is below 63 in the slots of the bin's own block (p // 768 = 4); in the other slots it takes every value up to 63.
All inputs are finite; a program needn't handle non-finite values.
Results may differ from the reference program's by a relative error of at most 0.0057.
Values may be sent and summed in bfloat16 or wider, within the bound.
A program may use at most 128 MiB of HBM per device.

```python
import math
import jax
import jax.numpy as jnp
from jax import lax

AUX = 1024
STATES = 8
VECS = 32
MOL_DEV = 64
CAP = 768
PAIRS = 6912
GRID_X = 8
GRID_Y = 4


def draw_pair_remote(key, part):
    owner = jnp.arange(PAIRS, dtype=jnp.int32) // CAP
    upper = jnp.where(owner == 4, MOL_DEV - 1, MOL_DEV).astype(jnp.int32)
    upper = jnp.broadcast_to(upper, (GRID_X, GRID_Y, PAIRS))
    return jax.random.randint(jax.random.fold_in(key, 17), (GRID_X, GRID_Y, PAIRS), 0, upper, dtype=jnp.int32)


def place_ends(result, stream_key, least, largest):
    extent = result.shape
    place = [jax.random.randint(jax.random.fold_in(stream_key, axis), (), 0, extent[axis]) for axis in range(len(extent))]
    result = result.at[tuple(place)].set(least)
    longest = extent.index(max(extent))
    place[longest] = (place[longest] + 1) % extent[longest]
    return result.at[tuple(place)].set(largest)


def level_of(own_key, shape, pieces, low, top_value):
    factor_of = 1.0
    for position, shards_of in pieces:
        steps = jax.random.uniform(jax.random.fold_in(jax.random.fold_in(own_key, 6), position), (shards_of,), jnp.float32, low / len(pieces), top_value / len(pieces))
        factor_of = factor_of * jnp.repeat(jnp.exp(steps), shape[position] // shards_of).reshape((-1,) + (1,) * (len(shape) - 1 - position))
    return factor_of


def noise(key, extent, deviation, most, cuts=(), kind=jnp.bfloat16):
    entries = deviation * jax.random.normal(key, extent, jnp.float32)
    if cuts:
        entries = entries * level_of(key, extent, cuts, -0.22, 0.18)
    return jnp.clip(entries, -most, most).astype(kind)


def setup_inputs(seed: int = 0) -> dict:
    key_list = jax.random.split(jax.random.key(seed), 8)
    return {
        "densities": noise(key_list[0], (GRID_X, GRID_Y, MOL_DEV, STATES * AUX), 1.0, 6.0, ((0, 8), (1, 4))),
        "trials": noise(key_list[1], (GRID_X, GRID_Y, MOL_DEV, STATES * VECS), 1.0, 6.0, ((0, 8), (1, 4))),
        "energies": jnp.clip(jnp.exp(math.log(4.0) - 1.3862944 * jax.random.uniform(key_list[2], (GRID_X, GRID_Y, MOL_DEV, STATES), jnp.float32) ** level_of(key_list[2], (GRID_X, GRID_Y, MOL_DEV, STATES), ((0, 8), (1, 4)), -0.2, 0.2)), 1.0, 4.0),
        "metric": noise(key_list[3], (AUX, AUX), AUX ** -0.5, 0.1875),
        "pair_local": place_ends(jax.random.randint(key_list[4], (GRID_X, GRID_Y, PAIRS), 0, MOL_DEV), jax.random.fold_in(key_list[4], 1), 0, MOL_DEV - 1).astype(jnp.int32),
        "pair_remote": draw_pair_remote(jax.random.fold_in(key_list[7], 71), 0),
        "pair_scale": jnp.clip(jnp.exp(math.log(2.0) - 2.3025851 * jax.random.uniform(key_list[6], (GRID_X, GRID_Y, PAIRS), jnp.float32) ** level_of(key_list[6], (GRID_X, GRID_Y, PAIRS), ((0, 8), (1, 4)), -0.2, 0.2)), 0.2, 2.0),
    }


def partner_index(bin_id, local, remote):
    bx = bin_id // GRID_Y
    by = bin_id % GRID_Y
    owner = jnp.arange(PAIRS, dtype=jnp.int32) // CAP
    nbin = (bx + owner // 3 - 1) % GRID_X * GRID_Y + (by + owner % 3 - 1) % GRID_Y
    inner = jnp.where(owner == 4, (local + 1 + remote) % MOL_DEV, remote)
    return (nbin * MOL_DEV + inner).astype(jnp.int32)

def reference(densities, trials, energies, metric, pair_local, pair_remote, pair_scale):
    nbins = GRID_X * GRID_Y
    flat_rho = densities.reshape(nbins * MOL_DEV, STATES, AUX)
    locals_all = pair_local.reshape(nbins, PAIRS)
    remotes_all = pair_remote.reshape(nbins, PAIRS)
    scales_all = pair_scale.reshape(nbins, PAIRS)
    bin_ids = jnp.arange(nbins, dtype=jnp.int32)
    index_all = jax.vmap(partner_index)(bin_ids, locals_all, remotes_all)
    energy_all = energies.reshape(nbins, MOL_DEV, STATES)

    def couple(items):
        bin_id, local, index, scale = items
        start = (bin_id * MOL_DEV).astype(jnp.int32)
        rho_bin = lax.dynamic_slice_in_dim(flat_rho, start, MOL_DEV, 0)
        proj = jnp.dot(rho_bin.reshape(MOL_DEV * STATES, AUX), metric, preferred_element_type=jnp.float32)
        proj = proj.astype(jnp.bfloat16).reshape(MOL_DEV, STATES, AUX)
        left = proj[local].astype(jnp.float32)
        right = flat_rho[index].astype(jnp.float32)
        block = jnp.einsum('pas,pbs->pab', left, right, precision=lax.Precision.HIGHEST)
        return block * (scale / jnp.sqrt(jnp.float32(AUX)))[:, None, None]
    couplings = lax.map(couple, (bin_ids, locals_all, index_all, scales_all))

    def matvec(field):
        flat = field.reshape(nbins * MOL_DEV, STATES, VECS)

        def one_bin(items):
            block, local, index, energy, own = items
            near = flat[index]
            contrib = jnp.einsum('pab,pbv->pav', block, near, precision=lax.Precision.HIGHEST)
            summed = jax.ops.segment_sum(contrib, local, MOL_DEV)
            return summed + energy[:, :, None] * own
        return lax.map(one_bin, (couplings, locals_all, index_all, energy_all, field))
    start_vecs = trials.astype(jnp.float32).reshape(nbins, MOL_DEV, STATES, VECS)
    sigma_first = matvec(start_vecs)
    numer = lax.optimization_barrier(jnp.sum(start_vecs * sigma_first, axis=(0, 1, 2)))
    denom = lax.optimization_barrier(jnp.sum(start_vecs * start_vecs, axis=(0, 1, 2)))
    theta = numer / denom
    resid = (sigma_first - theta * start_vecs) / jnp.maximum(jnp.abs(energy_all[:, :, :, None] - theta), 1.0)
    mean_sq = lax.optimization_barrier(jnp.sum(resid * resid, axis=(0, 1, 2))) / (nbins * MOL_DEV * STATES)
    corrections = (resid / jnp.sqrt(mean_sq + 1e-06)).astype(jnp.bfloat16)
    sigma_second = matvec(corrections.astype(jnp.float32))
    shape = (GRID_X, GRID_Y, MOL_DEV, STATES * VECS)
    return (sigma_first.reshape(shape), corrections.reshape(shape), sigma_second.reshape(shape), theta)
```

```python
import functools

import jax
import jax.numpy as jnp
from jax import lax
from jax.experimental import pallas as pl
from jax.experimental.pallas import tpu as pltpu
from jax.sharding import PartitionSpec as P

MESH = pl.DeviceIdType.MESH
NT = (((1,), (1,)), ((), ()))
LANES = 128
F32 = jnp.float32
BF16 = jnp.bfloat16


def kernel(
    nx, ny,
    rho, trial, energy, metric, plocal, premote, pscale,
    sigma_first, corr_out, sigma_second, theta_out,
    near, proj, c_own, c_low, c_left, c_right,
    w_own, w_send, w_low, w_side,
    y_near, r_send, r_near, ycat, ret_send, ret_near, sum_y, sum_x,
    rho_ss, rho_rs, small_ss, small_rs, ysum_ss, ysum_rs, xsum_ss, xsum_rs,
):
    mols, full = rho.shape[2], rho.shape[3]
    aux = metric.shape[0]
    states = full // aux
    vecs = trial.shape[3] // states
    width = mols * states
    cap = plocal.shape[2] // 9
    tile = c_left.shape[1] // 2
    me_x, me_y = lax.axis_index("gx"), lax.axis_index("gy")
    up = (lax.rem(me_x + 1, nx), me_y)
    down = (lax.rem(me_x + nx - 1, nx), me_y)
    right = (me_x, lax.rem(me_y + 1, ny))
    left = (me_x, lax.rem(me_y + ny - 1, ny))
    routes = ((right, 0), (left, 1), (up, 2))

    barrier = pltpu.get_barrier_semaphore()
    for k in range(1, ny):
        pl.semaphore_signal(barrier, inc=1, device_id=(me_x, lax.rem(me_y + k, ny)), device_id_type=MESH)
    for k in range(1, nx):
        pl.semaphore_signal(barrier, inc=1, device_id=(lax.rem(me_x + k, nx), me_y), device_id_type=MESH)
    pl.semaphore_wait(barrier, nx + ny - 2)

    pending = []

    def send(src, dst, ss, rs, target):
        copy = pltpu.make_async_remote_copy(
            src_ref=src, dst_ref=dst, send_sem=ss, recv_sem=rs, device_id=target, device_id_type=MESH
        )
        copy.start()
        pending.append(copy)
        return copy

    y_copies = [
        send(trial.at[0, 0], y_near.at[slot], small_ss.at[0, slot], small_rs.at[0, slot], target)
        for target, slot in routes
    ]
    rho_copies = [[None] * states for _ in range(3)]
    for a in range(states):
        for target, slot in routes:
            rho_copies[slot][a] = send(
                rho.at[0, 0, :, pl.ds(a * aux, aux)],
                near.at[pl.ds((slot + 1) * width + a * mols, mols), :],
                rho_ss.at[slot, a], rho_rs.at[slot, a], target,
            )

    norm = 1.0 / (float(aux) ** 0.5)
    ids = lax.broadcasted_iota(jnp.int32, (mols, cap), 0)

    def weight(o):
        span = pl.ds(o * cap, cap)
        mine = plocal[0, :, span]
        other = premote[0, :, span]
        if o == 4:
            other = mine + 1 + other
            other = jnp.where(other >= mols, other - mols, other)
        scale = pscale[0, :, span]
        high = scale.astype(BF16).astype(F32)
        low = scale - high
        hit = ids == mine
        own = jnp.concatenate([jnp.where(hit, high, 0.0), jnp.where(hit, low, 0.0)], axis=0).astype(BF16)
        far = jnp.where(ids == other, 1.0, 0.0)
        far = jnp.concatenate([far] * (LANES // mols), axis=0).astype(BF16)
        both = lax.dot_general(own, far, NT, preferred_element_type=F32)
        return (both[:mols] + both[mols:]) * norm

    for place, o in enumerate((7, 6, 8, 2, 0)):
        w_send[place] = weight(o)
    w_copies = [
        send(w_send.at[3], w_side.at[0], small_ss.at[1, 0], small_rs.at[1, 0], right),
        send(w_send.at[4], w_side.at[1], small_ss.at[1, 1], small_rs.at[1, 1], left),
        send(w_send.at[pl.ds(0, 3)], w_low, small_ss.at[1, 2], small_rs.at[1, 2], up),
    ]
    for place, o in enumerate((4, 3, 5, 1)):
        w_own[place] = weight(o)

    for a in range(states):
        near[pl.ds(a * mols, mols), :] = rho[0, 0, :, pl.ds(a * aux, aux)]

    def project(start, rows):
        @pl.loop(0, aux // 256)
        def _(i):
            cols = pl.ds(pl.multiple_of(i * 256, 256), 256)
            proj[pl.ds(start, rows), cols] = jnp.dot(
                near[pl.ds(start, rows), :], metric[:, cols], preferred_element_type=F32
            ).astype(BF16)

    def couple(out, out_start, proj_slot, near_start, w):
        dense = lax.dot_general(
            proj[pl.ds(proj_slot * width, width), :],
            near[pl.ds(near_start, tile), :],
            NT, preferred_element_type=F32,
        )
        wide = jnp.concatenate([w] * (tile // LANES), axis=1)
        dense = dense.reshape(states, mols, tile) * wide[None]
        out[:, pl.ds(out_start, tile)] = dense.reshape(width, tile).astype(BF16)

    project(0, width)

    @pl.loop(0, 2)
    def _(h):
        start = pl.multiple_of(h * tile, tile)
        couple(c_own, start, 0, start, w_own[0])

    def stacked(y):
        return jnp.concatenate([y[:, a * vecs:(a + 1) * vecs] for a in range(states)], axis=0)

    def merged(z):
        return jnp.concatenate([z[a * mols:(a + 1) * mols] for a in range(states)], axis=1)

    start_vecs = trial[0, 0].astype(F32)
    ycat[pl.ds(0, width), :] = stacked(start_vecs).astype(BF16)
    e = energy[0, 0]
    e_wide = jnp.concatenate(
        [jnp.broadcast_to(e[:, a:a + 1], (mols, vecs)) for a in range(states)], axis=1
    )
    for slot in range(3):
        y_copies[slot].wait_recv()
        ycat[pl.ds((slot + 1) * width, width), :] = stacked(y_near[slot].astype(F32)).astype(BF16)

    half = states // 2
    for h in range(2):
        for slot in range(3):
            for a in range(h * half, (h + 1) * half):
                rho_copies[slot][a].wait_recv()
            begin = (slot + 1) * width + h * tile
            project(begin, tile)
            couple(c_own, begin, 0, begin, w_own[slot + 1])
    for copy in w_copies:
        copy.wait_recv()

    @pl.loop(0, 6)
    def _(j):
        start = pl.multiple_of(j * tile, tile)
        couple(c_low, start, 3, start, w_low[j // 2])

    @pl.loop(0, 2)
    def _(h):
        start = pl.multiple_of(h * tile, tile)
        source = pl.multiple_of(3 * width + h * tile, tile)
        couple(c_left, start, 1, source, w_side[0])
        couple(c_right, start, 2, source, w_side[1])

    def apply(turn):
        for_low = jnp.dot(c_low[...], ycat[pl.ds(0, 3 * width), :], preferred_element_type=F32)
        last = ycat[pl.ds(3 * width, width), :]
        for_left = jnp.dot(c_left[...], last, preferred_element_type=F32)
        for_right = jnp.dot(c_right[...], last, preferred_element_type=F32)
        parts = [merged(for_left), merged(for_right), merged(for_low)]
        copies = []
        for slot, target in enumerate((left, right, down)):
            ret_send[turn, slot] = parts[slot]
            copies.append(send(
                ret_send.at[turn, slot], ret_near.at[turn, slot],
                small_ss.at[2 + turn, slot], small_rs.at[2 + turn, slot], target,
            ))
        own = merged(jnp.dot(c_own[...], ycat[...], preferred_element_type=F32))
        return own, parts, copies

    def total(turn, rows):
        block = jnp.concatenate(rows + [jnp.zeros((8 - len(rows), rows[0].shape[1]), F32)], axis=0)
        part = sum(block[:, i * LANES:(i + 1) * LANES] for i in range(block.shape[1] // LANES))
        shift = LANES // 2
        while shift >= vecs:
            part = part + pltpu.roll(part, shift, 1)
            shift //= 2
        for buf, ss, rs, me, count, at in (
            (sum_y, ysum_ss, ysum_rs, me_y, ny, lambda i: (me_x, i)),
            (sum_x, xsum_ss, xsum_rs, me_x, nx, lambda i: (i, me_y)),
        ):
            buf[turn, me] = part
            for k in range(1, count):
                send(buf.at[turn, me], buf.at[turn, me], ss.at[turn, k], rs.at[turn, me], at(lax.rem(me + k, count)))
            for k in range(1, count):
                source = lax.rem(me + k, count)
                pltpu.make_async_remote_copy(
                    src_ref=buf.at[turn, me], dst_ref=buf.at[turn, source],
                    send_sem=ss.at[turn, k], recv_sem=rs.at[turn, source],
                    device_id=at(source), device_id_type=MESH,
                ).wait_recv()
            part = buf[turn, 0]
            for i in range(1, count):
                part = part + buf[turn, i]
        return part

    def spread(row):
        return jnp.concatenate([row] * (states * vecs // LANES), axis=1)

    def over_mols(x):
        return jnp.sum(x, axis=0, keepdims=True)

    own, parts, copies = apply(0)
    own = own + e_wide * start_vecs
    inner = start_vecs * own
    for slot in range(3):
        inner = inner + y_near[slot].astype(F32) * parts[slot]
    sums = total(0, [over_mols(inner), over_mols(start_vecs * start_vecs)])
    theta = sums[0:1] / sums[1:2]
    theta_out[...] = theta[:, :vecs]
    theta = spread(theta)
    for slot in range(3):
        copies[slot].wait_recv()
        own = own + ret_near[0, slot]
    sigma_first[0, 0] = own
    resid = (own - theta * start_vecs) / jnp.maximum(jnp.abs(e_wide - theta), 1.0)
    r_send[...] = resid
    r_copies = [
        send(r_send, r_near.at[slot], small_ss.at[4, slot], small_rs.at[4, slot], target)
        for target, slot in routes
    ]
    sums = total(1, [over_mols(resid * resid)])
    factor = spread(1.0 / jnp.sqrt(sums[0:1] / (width * nx * ny) + 1e-6))
    corr = (resid * factor).astype(BF16)
    corr_out[0, 0] = corr
    corr = corr.astype(F32)
    ycat[pl.ds(0, width), :] = stacked(corr).astype(BF16)
    for slot in range(3):
        r_copies[slot].wait_recv()
        ycat[pl.ds((slot + 1) * width, width), :] = stacked(r_near[slot] * factor).astype(BF16)
    own, parts, copies = apply(1)
    own = own + e_wide * corr
    for slot in range(3):
        copies[slot].wait_recv()
        own = own + ret_near[1, slot]
    sigma_second[0, 0] = own
    for copy in pending:
        copy.wait_send()


def shards(densities, trials, energies, metric, pair_local, pair_remote, pair_scale):
    nx, ny = lax.axis_size("gx"), lax.axis_size("gy")
    mols = densities.shape[2]
    states = energies.shape[3]
    aux = metric.shape[0]
    vecs = trials.shape[3] // states
    width = mols * states
    field = (mols, states * vecs)
    vmem = pl.BlockSpec(memory_space=pltpu.VMEM)
    dma = pltpu.SemaphoreType.DMA
    s1, corr, s2, theta = pl.pallas_call(
        functools.partial(kernel, nx, ny),
        out_shape=(
            jax.ShapeDtypeStruct((1, 1) + field, F32),
            jax.ShapeDtypeStruct((1, 1) + field, BF16),
            jax.ShapeDtypeStruct((1, 1) + field, F32),
            jax.ShapeDtypeStruct((1, vecs), F32),
        ),
        in_specs=[vmem] * 7,
        out_specs=(vmem,) * 4,
        scratch_shapes=[
            pltpu.VMEM((4 * width, aux), BF16),
            pltpu.VMEM((4 * width, aux), BF16),
            pltpu.VMEM((width, 4 * width), BF16),
            pltpu.VMEM((width, 3 * width), BF16),
            pltpu.VMEM((width, width), BF16),
            pltpu.VMEM((width, width), BF16),
            pltpu.VMEM((4, mols, LANES), F32),
            pltpu.VMEM((5, mols, LANES), F32),
            pltpu.VMEM((3, mols, LANES), F32),
            pltpu.VMEM((2, mols, LANES), F32),
            pltpu.VMEM((3,) + field, BF16),
            pltpu.VMEM(field, F32),
            pltpu.VMEM((3,) + field, F32),
            pltpu.VMEM((4 * width, vecs), BF16),
            pltpu.VMEM((2, 3) + field, F32),
            pltpu.VMEM((2, 3) + field, F32),
            pltpu.VMEM((2, ny, 8, LANES), F32),
            pltpu.VMEM((2, nx, 8, LANES), F32),
            dma((3, states)), dma((3, states)),
            dma((5, 3)), dma((5, 3)),
            dma((2, ny)), dma((2, ny)),
            dma((2, nx)), dma((2, nx)),
        ],
        compiler_params=pltpu.CompilerParams(
            collective_id=0, has_side_effects=True, vmem_limit_bytes=48 * 1024 * 1024
        ),
    )(densities, trials, energies, metric, pair_local, pair_remote, pair_scale)
    return s1, corr, s2, theta.reshape(vecs)


def solution(mesh):
    field = P("gx", "gy", None, None)
    pair = P("gx", "gy", None)
    return jax.shard_map(
        shards,
        mesh=mesh,
        in_specs=(field, field, field, P(), pair, pair, pair),
        out_specs=(field, field, field, P()),
        check_vma=False,
    )
```

```python
import functools

import jax
import jax.numpy as jnp
from jax import lax
from jax.experimental import pallas as pl
from jax.experimental.pallas import tpu as pltpu
from jax.sharding import PartitionSpec as P

MESH = pl.DeviceIdType.MESH
NT = (((1,), (1,)), ((), ()))
LANES = 128
F32 = jnp.float32
BF16 = jnp.bfloat16


def kernel(
    nx, ny,
    rho_hbm, trial_hbm, energy_hbm, metric_hbm, plocal_hbm, premote_hbm, pscale_hbm,
    sigma_first, corr_out, sigma_second, theta_out,
    near, proj, c_own, c_low, c_side,
    trial, energy, metric, plocal, premote, pscale,
    w_own, w_send, w_low, w_side,
    y_near, r_send, r_near, ycat, ret_send, ret_near, last_send, last_near, sum_y, sum_x,
    rho_ss, rho_rs, small_ss, small_rs, ysum_ss, ysum_rs, xsum_ss, xsum_rs, load_s, own_s,
):
    mols, full = rho_hbm.shape[2], rho_hbm.shape[3]
    aux = metric.shape[0]
    states = full // aux
    tile = c_side.shape[1] // 2
    vecs = trial.shape[3] // states
    width = mols * states
    cap = plocal.shape[2] // 9
    me_x, me_y = lax.axis_index("gx"), lax.axis_index("gy")
    up = (lax.rem(me_x + 1, nx), me_y)
    down = (lax.rem(me_x + nx - 1, nx), me_y)
    right = (me_x, lax.rem(me_y + 1, ny))
    left = (me_x, lax.rem(me_y + ny - 1, ny))
    routes = ((right, 0), (left, 1), (up, 2))

    barrier = pltpu.get_barrier_semaphore()
    for k in range(1, ny):
        pl.semaphore_signal(barrier, inc=1, device_id=(me_x, lax.rem(me_y + k, ny)), device_id_type=MESH)
    for k in range(1, nx):
        pl.semaphore_signal(barrier, inc=1, device_id=(lax.rem(me_x + k, nx), me_y), device_id_type=MESH)

    loads = [
        pltpu.make_async_copy(src, dst, load_s.at[i])
        for i, (src, dst) in enumerate((
            (plocal_hbm, plocal), (premote_hbm, premote), (pscale_hbm, pscale),
            (trial_hbm, trial), (energy_hbm, energy), (metric_hbm, metric),
        ))
    ]
    own_loads = [
        pltpu.make_async_copy(
            rho_hbm.at[0, 0, :, pl.ds(a * aux, aux)], near.at[pl.ds(a * mols, mols), :], own_s.at[a]
        )
        for a in range(states)
    ]
    for load in own_loads + loads:
        load.start()
    pl.semaphore_wait(barrier, nx + ny - 2)

    pending = []

    def send(src, dst, ss, rs, target):
        copy = pltpu.make_async_remote_copy(
            src_ref=src, dst_ref=dst, send_sem=ss, recv_sem=rs, device_id=target, device_id_type=MESH
        )
        copy.start()
        pending.append(copy)
        return copy

    y_copies = [
        send(trial_hbm.at[0, 0], y_near.at[slot], small_ss.at[0, slot], small_rs.at[0, slot], target)
        for target, slot in routes
    ]
    rho_copies = [[None] * states for _ in range(3)]
    for a in range(states):
        own_loads[a].wait()
        for target, slot in routes:
            rho_copies[slot][a] = send(
                near.at[pl.ds(a * mols, mols), :],
                near.at[pl.ds((slot + 1) * width + a * mols, mols), :],
                rho_ss.at[slot, a], rho_rs.at[slot, a], target,
            )

    for load in loads[:3]:
        load.wait()
    norm = 1.0 / (float(aux) ** 0.5)
    ids = lax.broadcasted_iota(jnp.int32, (mols, cap), 0)

    def weight(o):
        span = pl.ds(o * cap, cap)
        mine = plocal[0, :, span]
        other = premote[0, :, span]
        if o == 4:
            other = mine + 1 + other
            other = jnp.where(other >= mols, other - mols, other)
        scale = pscale[0, :, span]
        high = scale.astype(BF16).astype(F32)
        low = scale - high
        hit = ids == mine
        own = jnp.concatenate([jnp.where(hit, high, 0.0), jnp.where(hit, low, 0.0)], axis=0).astype(BF16)
        far = jnp.where(ids == other, 1.0, 0.0)
        far = jnp.concatenate([far] * (LANES // mols), axis=0).astype(BF16)
        both = lax.dot_general(own, far, NT, preferred_element_type=F32)
        return (both[:mols] + both[mols:]) * norm

    for place, o in enumerate((7, 6, 8, 2, 0)):
        w_send[place] = weight(o)
    w_copies = [
        send(w_send.at[3], w_side.at[0], small_ss.at[1, 0], small_rs.at[1, 0], right),
        send(w_send.at[4], w_side.at[1], small_ss.at[1, 1], small_rs.at[1, 1], left),
        send(w_send.at[pl.ds(0, 3)], w_low, small_ss.at[1, 2], small_rs.at[1, 2], up),
    ]
    for place, o in enumerate((4, 3, 5, 1)):
        w_own[place] = weight(o)

    for load in loads[3:]:
        load.wait()

    def project(start, rows):
        @pl.loop(0, aux // 256)
        def _(i):
            cols = pl.ds(pl.multiple_of(i * 256, 256), 256)
            proj[pl.ds(start, rows), cols] = jnp.dot(
                near[pl.ds(start, rows), :], metric[:, cols], preferred_element_type=F32
            ).astype(BF16)

    def couple(out, out_start, proj_slot, near_start, w):
        dense = lax.dot_general(
            proj[pl.ds(proj_slot * width, width), :],
            near[pl.ds(near_start, tile), :],
            NT, preferred_element_type=F32,
        )
        wide = jnp.concatenate([w] * (tile // LANES), axis=1)
        dense = dense.reshape(states, mols, tile) * wide[None]
        out[:, pl.ds(out_start, tile)] = dense.reshape(width, tile).astype(BF16)

    project(0, width)

    @pl.loop(0, 2)
    def _(h):
        start = pl.multiple_of(h * tile, tile)
        couple(c_own, start, 0, start, w_own[0])

    def stacked(y):
        return jnp.concatenate([y[:, a * vecs:(a + 1) * vecs] for a in range(states)], axis=0)

    def merged(z):
        return jnp.concatenate([z[a * mols:(a + 1) * mols] for a in range(states)], axis=1)

    start_vecs = trial[0, 0].astype(F32)
    ycat[pl.ds(0, width), :] = stacked(start_vecs).astype(BF16)
    e = energy[0, 0].T
    e_wide = jnp.concatenate(
        [jnp.broadcast_to(e[:, a:a + 1], (mols, vecs)) for a in range(states)], axis=1
    )
    for slot in range(3):
        y_copies[slot].wait_recv()
        ycat[pl.ds((slot + 1) * width, width), :] = stacked(y_near[slot].astype(F32)).astype(BF16)

    half = states // 2
    for h in range(2):
        for slot in range(3):
            for a in range(h * half, (h + 1) * half):
                rho_copies[slot][a].wait_recv()
            begin = (slot + 1) * width + h * tile
            project(begin, tile)
            couple(c_own, begin, 0, begin, w_own[slot + 1])
    for copy in w_copies:
        copy.wait_recv()

    @pl.loop(0, 6)
    def _(j):
        start = pl.multiple_of(j * tile, tile)
        couple(c_low, start, 3, start, w_low[j // 2])

    @pl.loop(0, 2)
    def _(h):
        start = pl.multiple_of(h * tile, tile)
        source = pl.multiple_of(3 * width + h * tile, tile)
        couple(c_side.at[0], start, 1, source, w_side[0])
        couple(c_side.at[1], start, 2, source, w_side[1])

    def apply(turn):
        for_low = jnp.dot(c_low[...], ycat[pl.ds(0, 3 * width), :], preferred_element_type=F32)
        last = ycat[pl.ds(3 * width, width), :]
        for_left = jnp.dot(c_side[0], last, preferred_element_type=F32)
        for_right = jnp.dot(c_side[1], last, preferred_element_type=F32)
        parts = [merged(for_left), merged(for_right), merged(for_low)]
        copies = []
        for slot, target in enumerate((left, right, down)):
            src, dst = ((ret_send, ret_near), (last_send, last_near))[turn]
            src[slot] = parts[slot].astype(src.dtype)
            copies.append(send(
                src.at[slot], dst.at[slot],
                small_ss.at[2 + turn, slot], small_rs.at[2 + turn, slot], target,
            ))
        own = merged(jnp.dot(c_own[...], ycat[...], preferred_element_type=F32))
        return own, parts, copies

    def total(turn, rows):
        block = jnp.concatenate(rows + [jnp.zeros((8 - len(rows), rows[0].shape[1]), F32)], axis=0)
        part = sum(block[:, i * LANES:(i + 1) * LANES] for i in range(block.shape[1] // LANES))
        shift = LANES // 2
        while shift >= vecs:
            part = part + pltpu.roll(part, shift, 1)
            shift //= 2
        for buf, ss, rs, me, count, at in (
            (sum_y, ysum_ss, ysum_rs, me_y, ny, lambda i: (me_x, i)),
            (sum_x, xsum_ss, xsum_rs, me_x, nx, lambda i: (i, me_y)),
        ):
            buf[turn, me] = part
            for k in range(1, count):
                send(buf.at[turn, me], buf.at[turn, me], ss.at[turn, k], rs.at[turn, me], at(lax.rem(me + k, count)))
            for k in range(1, count):
                source = lax.rem(me + k, count)
                pltpu.make_async_remote_copy(
                    src_ref=buf.at[turn, me], dst_ref=buf.at[turn, source],
                    send_sem=ss.at[turn, k], recv_sem=rs.at[turn, source],
                    device_id=at(source), device_id_type=MESH,
                ).wait_recv()
            part = buf[turn, 0]
            for i in range(1, count):
                part = part + buf[turn, i]
        return part

    def spread(row):
        return jnp.concatenate([row] * (states * vecs // LANES), axis=1)

    def over_mols(x):
        return jnp.sum(x, axis=0, keepdims=True)

    own, parts, copies = apply(0)
    own = own + e_wide * start_vecs
    inner = start_vecs * own
    for slot in range(3):
        inner = inner + y_near[slot].astype(F32) * parts[slot]
    sums = total(0, [over_mols(inner), over_mols(start_vecs * start_vecs)])
    theta = sums[0:1] / sums[1:2]
    theta_out[...] = theta[:, :vecs]
    theta = spread(theta)
    for slot in range(3):
        copies[slot].wait_recv()
        own = own + ret_near[slot]
    sigma_first[0, 0] = own
    resid = (own - theta * start_vecs) / jnp.maximum(jnp.abs(e_wide - theta), 1.0)
    r_send[...] = resid
    r_copies = [
        send(r_send, r_near.at[slot], small_ss.at[4, slot], small_rs.at[4, slot], target)
        for target, slot in routes
    ]
    sums = total(1, [over_mols(resid * resid)])
    factor = spread(1.0 / jnp.sqrt(sums[0:1] / (width * nx * ny) + 1e-6))
    corr = (resid * factor).astype(BF16)
    corr_out[0, 0] = corr
    corr = corr.astype(F32)
    ycat[pl.ds(0, width), :] = stacked(corr).astype(BF16)
    for slot in range(3):
        r_copies[slot].wait_recv()
        ycat[pl.ds((slot + 1) * width, width), :] = stacked(r_near[slot] * factor).astype(BF16)
    own, parts, copies = apply(1)
    own = own + e_wide * corr
    for slot in range(3):
        copies[slot].wait_recv()
        own = own + last_near[slot].astype(F32)
    sigma_second[0, 0] = own
    for copy in pending:
        copy.wait_send()


def shards(densities, trials, energies, metric, pair_local, pair_remote, pair_scale):
    nx, ny = lax.axis_size("gx"), lax.axis_size("gy")
    mols = densities.shape[2]
    states = energies.shape[3]
    aux = metric.shape[0]
    vecs = trials.shape[3] // states
    width = mols * states
    field = (mols, states * vecs)
    vmem = pl.BlockSpec(memory_space=pltpu.VMEM)
    hbm = pl.BlockSpec(memory_space=pltpu.HBM)
    flipped = jnp.swapaxes(energies, 2, 3)
    dma = pltpu.SemaphoreType.DMA
    s1, corr, s2, theta = pl.pallas_call(
        functools.partial(kernel, nx, ny),
        out_shape=(
            jax.ShapeDtypeStruct((1, 1) + field, F32),
            jax.ShapeDtypeStruct((1, 1) + field, BF16),
            jax.ShapeDtypeStruct((1, 1) + field, F32),
            jax.ShapeDtypeStruct((1, vecs), F32),
        ),
        in_specs=[hbm] * 7,
        out_specs=(vmem,) * 4,
        scratch_shapes=[
            pltpu.VMEM((4 * width, aux), BF16),
            pltpu.VMEM((4 * width, aux), BF16),
            pltpu.VMEM((width, 4 * width), BF16),
            pltpu.VMEM((width, 3 * width), BF16),
            pltpu.VMEM((2, width, width), BF16),
            pltpu.VMEM(trials.shape, trials.dtype),
            pltpu.VMEM(flipped.shape, flipped.dtype),
            pltpu.VMEM(metric.shape, metric.dtype),
            pltpu.VMEM(pair_local.shape, pair_local.dtype),
            pltpu.VMEM(pair_remote.shape, pair_remote.dtype),
            pltpu.VMEM(pair_scale.shape, pair_scale.dtype),
            pltpu.VMEM((4, mols, LANES), F32),
            pltpu.VMEM((5, mols, LANES), F32),
            pltpu.VMEM((3, mols, LANES), F32),
            pltpu.VMEM((2, mols, LANES), F32),
            pltpu.VMEM((3,) + field, BF16),
            pltpu.VMEM(field, F32),
            pltpu.VMEM((3,) + field, F32),
            pltpu.VMEM((4 * width, vecs), BF16),
            pltpu.VMEM((3,) + field, F32),
            pltpu.VMEM((3,) + field, F32),
            pltpu.VMEM((3,) + field, BF16),
            pltpu.VMEM((3,) + field, BF16),
            pltpu.VMEM((2, ny, 8, LANES), F32),
            pltpu.VMEM((2, nx, 8, LANES), F32),
            dma((3, states)), dma((3, states)),
            dma((5, 3)), dma((5, 3)),
            dma((2, ny)), dma((2, ny)),
            dma((2, nx)), dma((2, nx)),
            dma((6,)), dma((states,)),
        ],
        compiler_params=pltpu.CompilerParams(
            collective_id=0, has_side_effects=True, vmem_limit_bytes=62 * 1024 * 1024
        ),
    )(densities, trials, flipped, metric, pair_local, pair_remote, pair_scale)
    return s1, corr, s2, theta.reshape(vecs)


def solution(mesh):
    field = P("gx", "gy", None, None)
    pair = P("gx", "gy", None)
    return jax.shard_map(
        shards,
        mesh=mesh,
        in_specs=(field, field, field, P(), pair, pair, pair),
        out_specs=(field, field, field, P()),
        check_vma=False,
    )
```
